32 devices in a mesh: ka: 4 (over x, core), grid: 8 (over z, y).
Axes of the slice: x: 2, y: 2, z: 4, core: 2. Of those that a mesh axis runs over, the one named last changes fastest.
Arguments:
- orbitals: bfloat16 [4, 2, 512, 8192], P('ka', None, None, 'grid'), may hold values from -6 to 6
- potential: float32 [3, 2, 8192], P(None, None, 'grid'), may hold values from -6 to 6
- partners: int32 [3, 4], replicated, may hold values from 0 to 3, each once within a row
- occupied: int32 [4], replicated, may hold values from 128 to 512
Outputs:
- sources: bfloat16 [3, 4, 2, 512, 8192], P(None, 'ka', None, None, 'grid')
- density: float32 [3, 8192], P(None, 'grid')
The draws below stay inside these ranges and needn't reach their ends.
Inputs may be any that keep to these rules, and one draw needn't show every extreme that they name: `partners`: each row is a permutation of the 4 k-points.
All inputs are finite; a program needn't handle non-finite values.
Results may differ from the reference program's by a relative error of at most 0.0051.
Values may be sent and summed in bfloat16 or wider, within the bound.
No kernel may reach another device: no remote copies, remote signals or barrier semaphores. Data moves between devices by JAX's collectives and lax.ppermute only.
A program may use at most 128 MiB of HBM per device.

```python
import jax
import jax.numpy as jnp
from jax import lax

BANDS = 512
Q = 3
K = 4
GRID = 8192


def with_ends(result, own_key, smallest, high):
    place = [jax.random.randint(jax.random.fold_in(own_key, axis), (), 0, length) for axis, length in enumerate(result.shape)]
    longest = result.shape.index(max(result.shape))
    beside = place[:longest] + [(place[longest] + 1) % result.shape[longest]] + place[longest + 1:]
    return result.at[tuple(place)].set(smallest).at[tuple(beside)].set(high)


def level_of(stream_key, extent, split, smallest, high):
    loudness = 1.0
    for dim, shards_of in split:
        draws = jax.random.uniform(jax.random.fold_in(jax.random.fold_in(stream_key, 6), dim), (shards_of,), jnp.float32, smallest / len(split), high / len(split))
        loudness = loudness * jnp.repeat(jnp.exp(draws), extent[dim] // shards_of).reshape((-1,) + (1,) * (len(extent) - 1 - dim))
    return loudness


def noise(key, dims, scale, limit, split=(), kind=jnp.bfloat16):
    entries = scale * jax.random.normal(key, dims, jnp.float32)
    if split:
        entries = entries * level_of(key, dims, split, -0.22, 0.18)
    return jnp.clip(entries, -limit, limit).astype(kind)


def setup_inputs(seed: int = 0) -> dict:
    seeds = jax.random.split(jax.random.key(seed), 5)
    return {
        "orbitals": noise(seeds[0], (K, 2, BANDS, GRID), 1.0, 6.0, ((0, 4), (3, 8))),
        "potential": noise(seeds[1], (Q, 2, GRID), 1.0, 6.0, ((2, 8),), jnp.float32),
        "partners": jax.vmap(lambda own: jax.random.permutation(own, K))(jax.random.split(seeds[2], Q)).reshape((Q, K)).astype(jnp.int32),
        "occupied": with_ends(jax.random.randint(seeds[3], (K,), BANDS // 4, BANDS + 1), jax.random.fold_in(seeds[3], 1), BANDS // 4, BANDS).astype(jnp.int32),
    }


def reference(orbitals, potential, partners, occupied):
    volume_weight = 1.0 / GRID
    density_weight = 2.0 / (K * BANDS)
    band_ids = jnp.arange(BANDS, dtype=jnp.int32)
    all_sources = []
    all_density = []
    for q_index in range(Q):
        real_field = potential[q_index, 0]
        imag_field = potential[q_index, 1]

        def per_point(k_index):
            partner = partners[q_index, k_index]
            own_orbit = orbitals[k_index].astype(jnp.float32)
            partner_orbit = orbitals[partner].astype(jnp.float32)
            applied_real = real_field * own_orbit[0] - imag_field * own_orbit[1]
            applied_imag = real_field * own_orbit[1] + imag_field * own_orbit[0]
            rounded = lax.optimization_barrier(jnp.stack([applied_real, applied_imag]).astype(jnp.bfloat16))
            applied = rounded.astype(jnp.float32)
            swapped = jnp.stack([applied[1], -applied[0]])
            over_real = volume_weight * jnp.einsum("cmg,cng->mn", partner_orbit, applied)
            over_imag = volume_weight * jnp.einsum("cmg,cng->mn", partner_orbit, swapped)
            partner_mask = (band_ids < occupied[partner]).astype(jnp.float32)[:, None]
            masked = lax.optimization_barrier(jnp.stack([over_real * partner_mask, over_imag * partner_mask]).astype(jnp.bfloat16))
            masked = masked.astype(jnp.float32)
            weight_real = jnp.stack([masked[0], -masked[1]])
            weight_imag = jnp.stack([masked[1], masked[0]])
            projected_real = applied[0] - jnp.einsum("cmg,cmn->ng", partner_orbit, weight_real)
            projected_imag = applied[1] - jnp.einsum("cmg,cmn->ng", partner_orbit, weight_imag)
            source_block = jnp.stack([projected_real, projected_imag]).astype(jnp.bfloat16)
            own_mask = (band_ids < occupied[k_index]).astype(jnp.float32)[:, None]
            density_term = jnp.sum(own_mask * (own_orbit[0] * projected_real + own_orbit[1] * projected_imag), axis=0)
            return source_block, density_term

        source_blocks, density_terms = lax.map(per_point, jnp.arange(K, dtype=jnp.int32))
        all_sources.append(source_blocks)
        all_density.append(density_weight * jnp.sum(density_terms, axis=0))
    return jnp.stack(all_sources), jnp.stack(all_density)
```

```python
import functools

import jax
import jax.numpy as jnp
from jax import lax
from jax.experimental import pallas as pl
from jax.experimental.pallas import tpu as pltpu
from jax.sharding import PartitionSpec as P

VMEM_LIMIT = 56 * 1024 * 1024
PLAN = ((0, 2, "all"), (2, 4, "each"))


def swap(value, axis, bit):
    size = lax.axis_size(axis)
    return lax.ppermute(value, axis, [(i, i ^ bit) for i in range(size)])


def axis_bits(axis):
    size = lax.axis_size(axis)
    return [1 << b for b in range(size.bit_length() - 1)]


def apply_field(orbitals, potential):
    real = orbitals[0].astype(jnp.float32)
    imag = orbitals[1].astype(jnp.float32)
    u = potential[:, 0][:, None, :]
    v = potential[:, 1][:, None, :]
    return jnp.stack([u * real - v * imag, u * imag + v * real], axis=1).astype(jnp.bfloat16)


def nt_dot(left, right):
    return lax.dot_general(left, right, (((1,), (1,)), ((), ())), preferred_element_type=jnp.float32)


def overlap(applied_ref, partner, out_ref):
    a_real, a_imag = applied_ref[0, 0], applied_ref[0, 1]
    p_real, p_imag = partner[0], partner[1]
    out_ref[0, 0] = (nt_dot(a_real, p_real) + nt_dot(a_imag, p_imag)).astype(out_ref.dtype)
    out_ref[0, 1] = (nt_dot(a_imag, p_real) - nt_dot(a_real, p_imag)).astype(out_ref.dtype)


def send_kernel(count, picks_ref, half_ref, applied_ref, *refs):
    sources, (out_ref, pick_ref) = refs[:count], refs[count:]
    pick = picks_ref[pl.program_id(0)]
    for j in range(count):
        @pl.when(pick == j)
        def _():
            pick_ref[0] = sources[j][...]
    overlap(applied_ref, pick_ref[0], out_ref)


def keep_kernel(half_ref, applied_ref, pick_ref, out_ref):
    overlap(applied_ref, pick_ref[0], out_ref)


def overlap_send(q0, q_count, start, picks, half, applied, sources):
    _, _, bands, points = applied.shape
    width = sources[-1][0].shape[1]
    rows = bands // 2
    specs = []
    for array, is_whole in sources:
        row = start // width if is_whole else 0
        specs.append(pl.BlockSpec((2, width, points), lambda q, p, h, row=row: (0, row, 0), pipeline_mode=pl.Buffered(1)))
    return pl.pallas_call(
        functools.partial(send_kernel, len(sources)),
        grid_spec=pltpu.PrefetchScalarGridSpec(
            num_scalar_prefetch=2,
            grid=(q_count,),
            in_specs=[pl.BlockSpec((1, 2, rows, points), lambda q, p, h: (q0 + q, 0, h[0], 0))] + specs,
            out_specs=[
                pl.BlockSpec((1, 2, rows, width), lambda q, p, h: (q, 0, 0, 0)),
                pl.BlockSpec((1, 2, width, points), lambda q, p, h: (q, 0, 0, 0)),
            ],
        ),
        out_shape=[
            jax.ShapeDtypeStruct((q_count, 2, rows, width), jnp.bfloat16),
            jax.ShapeDtypeStruct((q_count, 2, width, points), jnp.bfloat16),
        ],
        compiler_params=pltpu.CompilerParams(vmem_limit_bytes=VMEM_LIMIT),
        cost_estimate=pl.CostEstimate(
            flops=8 * q_count * rows * width * points,
            bytes_accessed=q_count * 4 * points * (rows + width) + 4 * len(sources) * width * points,
            transcendentals=0,
        ),
    )(picks, half, applied, *[array for array, _ in sources])


def overlap_keep(q0, half, applied, picked):
    q_count, _, width, points = picked.shape
    rows = applied.shape[2] // 2
    return pl.pallas_call(
        keep_kernel,
        grid_spec=pltpu.PrefetchScalarGridSpec(
            num_scalar_prefetch=1,
            grid=(q_count,),
            in_specs=[
                pl.BlockSpec((1, 2, rows, points), lambda q, h: (q0 + q, 0, h[0], 0)),
                pl.BlockSpec((1, 2, width, points), lambda q, h: (q, 0, 0, 0)),
            ],
            out_specs=pl.BlockSpec((1, 2, rows, width), lambda q, h: (q, 0, 0, 0)),
        ),
        out_shape=jax.ShapeDtypeStruct((q_count, 2, rows, width), jnp.float32),
        compiler_params=pltpu.CompilerParams(vmem_limit_bytes=VMEM_LIMIT),
        cost_estimate=pl.CostEstimate(
            flops=8 * q_count * rows * width * points,
            bytes_accessed=q_count * 4 * points * (rows + width),
            transcendentals=0,
        ),
    )(half, applied, picked)


def mix_kernel(chunk_count, weight_scale, count_ref, applied_ref, own_ref, *refs):
    weights = refs[:chunk_count]
    partners = refs[chunk_count:2 * chunk_count]
    source_ref, density_ref = refs[-2:]
    block = own_ref.shape[1]
    real = applied_ref[0, 0].astype(jnp.float32)
    imag = applied_ref[0, 1].astype(jnp.float32)
    for weight, partner in zip(weights, partners):
        w_real, w_imag = weight[0, 0], weight[0, 1]
        p_real, p_imag = partner[0, 0], partner[0, 1]
        real -= jnp.dot(w_real, p_real, preferred_element_type=jnp.float32)
        real += jnp.dot(w_imag, p_imag, preferred_element_type=jnp.float32)
        imag -= jnp.dot(w_imag, p_real, preferred_element_type=jnp.float32)
        imag -= jnp.dot(w_real, p_imag, preferred_element_type=jnp.float32)
    source_ref[0, 0, 0] = real.astype(jnp.bfloat16)
    source_ref[0, 0, 1] = imag.astype(jnp.bfloat16)
    term = own_ref[0].astype(jnp.float32) * real + own_ref[1].astype(jnp.float32) * imag
    ids = pl.program_id(0) * block + lax.broadcasted_iota(jnp.int32, (block, 1), 0)
    term = jnp.where(ids < count_ref[0], term, 0.0)
    total = weight_scale * jnp.sum(term, axis=0, keepdims=True)

    @pl.when(pl.program_id(0) == 0)
    def _():
        density_ref[...] = jnp.zeros_like(density_ref)

    density_ref[...] += total


def mix(q, count, applied, orbitals, weights, partners, buffer, weight_scale):
    q_total, _, bands, points = applied.shape
    block = bands // 4
    n = len(weights)
    specs = [
        pl.BlockSpec((1, 2, block, points), lambda i, c: (q, 0, i, 0)),
        pl.BlockSpec((2, block, points), lambda i, c: (0, i, 0)),
    ]
    arrays = [applied, orbitals]
    for at, weight in weights:
        specs.append(pl.BlockSpec((1, 2, block, weight.shape[3]), lambda i, c, at=at: (at, 0, i, 0)))
        arrays.append(weight)
    for at, partner in partners:
        specs.append(pl.BlockSpec((1,) + partner.shape[1:], lambda i, c, at=at: (at, 0, 0, 0)))
        arrays.append(partner)
    aliases = {}
    if buffer is not None:
        specs.append(pl.BlockSpec(memory_space=pl.ANY))
        arrays.append(buffer)
        aliases = {len(arrays): 0}
    return pl.pallas_call(
        functools.partial(mix_kernel, n, weight_scale),
        grid_spec=pltpu.PrefetchScalarGridSpec(
            num_scalar_prefetch=1,
            grid=(bands // block,),
            in_specs=specs,
            out_specs=[
                pl.BlockSpec((1, 1, 2, block, points), lambda i, c: (q, 0, 0, i, 0)),
                pl.BlockSpec((1, points), lambda i, c: (0, 0)),
            ],
        ),
        out_shape=[
            jax.ShapeDtypeStruct((q_total, 1, 2, bands, points), jnp.bfloat16),
            jax.ShapeDtypeStruct((1, points), jnp.float32),
        ],
        input_output_aliases=aliases,
        compiler_params=pltpu.CompilerParams(vmem_limit_bytes=VMEM_LIMIT),
        cost_estimate=pl.CostEstimate(
            flops=8 * bands * bands * points, bytes_accessed=16 * bands * points, transcendentals=0
        ),
    )(count, *arrays)


def shards(orbitals, potential, partners, occupied):
    own = orbitals[0]
    bands, points = own.shape[1:]
    q_count = potential.shape[0]
    k_count = partners.shape[1]
    k_index = lax.axis_index("ka")
    g_index = lax.axis_index("grid")
    ka_bits = axis_bits("ka")[::-1]
    grid_bits = axis_bits("grid")
    volume_weight = 1.0 / (points * lax.axis_size("grid"))
    density_weight = 2.0 / (k_count * bands)
    k_table = jnp.arange(k_count, dtype=jnp.int32)
    partner_ids = jnp.sum((k_table == k_index) * partners, axis=1)
    partner_counts = jnp.sum((partner_ids[:, None] == k_table[None, :]) * occupied[None, :], axis=1)
    own_count = jnp.sum((k_table == k_index) * occupied)[None]
    picks = partner_ids ^ k_index

    sent = []
    for first, last, _ in PLAN:
        start, stop = first * bands // 4, last * bands // 4
        have = {0: own[:, start:stop]}
        for bit in ka_bits[:-1]:
            for rel in list(have):
                have[rel ^ bit] = swap(have[rel], "ka", bit)
        sent.append((start, stop, have))
    sibling = swap(own, "ka", ka_bits[-1])
    applied = apply_field(own, potential)

    def bit_of(bit):
        return (g_index // bit) % 2

    first_bit = bit_of(grid_bits[0])
    keep_half = first_bit[None].astype(jnp.int32)
    send_half = 1 - keep_half

    def reduce_scatter(keep, arriving):
        for bit in grid_bits[1:]:
            mine = bit_of(bit)
            half = keep.shape[2] // 2

            def part(which):
                return lax.dynamic_slice_in_dim(keep, which * half, half, 2) + lax.dynamic_slice_in_dim(
                    arriving, which * half, half, 2
                ).astype(jnp.float32)

            leaving = part(1 - mine).astype(jnp.bfloat16)
            keep, arriving = part(mine), swap(leaving, "grid", bit)
        return keep + arriving.astype(jnp.float32)

    def all_gather(piece):
        for bit in grid_bits[::-1]:
            other = swap(piece, "grid", bit)
            upper = bit_of(bit) == 1
            piece = jnp.concatenate([jnp.where(upper, other, piece), jnp.where(upper, piece, other)], axis=2)
        return piece

    weights = [[] for _ in range(q_count)]
    picked = [[] for _ in range(q_count)]
    for (start, stop, have), (_, _, mode) in zip(sent, PLAN):
        for rel in list(have):
            if rel:
                have[rel ^ ka_bits[-1]] = swap(have[rel], "ka", ka_bits[-1])
        have[ka_bits[-1]] = None
        sources = []
        for rel in range(len(have)):
            whole = {0: own, ka_bits[-1]: sibling}.get(rel)
            sources.append((have[rel], False) if whole is None else (whole, True))
        groups = [(0, q_count)] if mode == "all" else [(q, 1) for q in range(q_count)]
        for q0, count in groups:
            leaving, chosen = overlap_send(q0, count, start, picks[q0:q0 + count], send_half, applied, sources)
            arriving = swap(leaving, "grid", grid_bits[0])
            keep = overlap_keep(q0, keep_half, applied, chosen)
            total = reduce_scatter(keep, arriving)
            limits = partner_counts[q0:q0 + count][:, None, None, None]
            mask = (start + jnp.arange(stop - start, dtype=jnp.int32)) < limits
            piece = jnp.where(mask, volume_weight * total, 0.0).astype(jnp.bfloat16)
            whole = all_gather(piece)
            for q in range(q0, q0 + count):
                weights[q].append((q - q0, whole))
                picked[q].append((q - q0, chosen))

    buffer = None
    density = []
    for q in range(q_count):
        buffer, term = mix(q, own_count, applied, own, weights[q], picked[q], buffer, density_weight)
        density.append(term)
    density = jnp.concatenate(density, axis=0)
    parts = [density] + [swap_by(density, d) for d in range(1, lax.axis_size("ka"))]
    while len(parts) > 1:
        half = len(parts) // 2
        parts = [parts[i] + parts[i + half] for i in range(half)]
    return buffer, parts[0]


def swap_by(value, distance):
    return swap(value, "ka", distance)


def solution(mesh):
    return jax.shard_map(
        shards,
        mesh=mesh,
        in_specs=(P("ka", None, None, "grid"), P(None, None, "grid"), P(), P()),
        out_specs=(P(None, "ka", None, None, "grid"), P(None, "grid")),
        check_vma=False,
    )
```

```python
import functools

import jax
import jax.numpy as jnp
from jax import lax
from jax.experimental import pallas as pl
from jax.experimental.pallas import tpu as pltpu
from jax.sharding import PartitionSpec as P

SMALL_COST = pl.CostEstimate(flops=1, bytes_accessed=1, transcendentals=0)
VMEM_LIMIT = 24 * 1024 * 1024
LAG = 0.3
PACE = 0.6
PLAN = ((0, 1, True), (1, 1, True), (2, 1, True), (3, 1, True))


def swap(value, axis, bit):
    size = lax.axis_size(axis)
    return lax.ppermute(value, axis, [(i, i ^ bit) for i in range(size)])


def after(value, *others):
    return lax.optimization_barrier((value,) + others)[0]


def axis_bits(axis):
    size = lax.axis_size(axis)
    return [1 << b for b in range(size.bit_length() - 1)]


def overlap_kernel(count, picks_ref, half_ref, own_ref, field_ref, *refs):
    sources = refs[:count]
    send_ref, keep_ref, pick_ref, full, turned = refs[-5:]
    pick = picks_ref[pl.program_id(0)]
    for j in range(count):
        @pl.when(pick == j)
        def _():
            pick_ref[0] = sources[j][...]
    _, bands, points = own_ref.shape
    width = pick_ref.shape[2]
    rows = bands // 2
    u, v = field_ref[0, 0:1], field_ref[0, 1:2]
    p_real, p_imag = pick_ref[0, 0].astype(jnp.float32), pick_ref[0, 1].astype(jnp.float32)
    turned[:width] = (u * p_real + v * p_imag).astype(jnp.bfloat16)
    turned[width:] = (u * p_imag - v * p_real).astype(jnp.bfloat16)
    both = lax.dot_general(
        own_ref[...].reshape(2 * bands, points),
        turned[...],
        (((1,), (1,)), ((), ())),
        preferred_element_type=jnp.float32,
    )
    full[0] = both[:bands, :width] + both[bands:, width:]
    full[1] = both[bands:, :width] - both[:bands, width:]
    away = pl.multiple_of(half_ref[0] * rows, rows)
    here = pl.multiple_of((1 - half_ref[0]) * rows, rows)
    send_ref[0] = full[:, pl.ds(away, rows), :].astype(send_ref.dtype)
    keep_ref[0] = full[:, pl.ds(here, rows), :]


def overlap(q0, q_count, start, picks, half, own, potential, sources):
    _, bands, points = own.shape
    width = sources[-1][0].shape[1]
    rows = bands // 2
    chunk = start // width
    specs = []
    for array, is_whole in sources:
        row = chunk if is_whole else 0
        specs.append(pl.BlockSpec((2, width, points), lambda q, p, h, row=row: (0, row, 0), pipeline_mode=pl.Buffered(1)))
    arrays = [own, potential] + [array for array, _ in sources]
    return pl.pallas_call(
        functools.partial(overlap_kernel, len(sources)),
        grid_spec=pltpu.PrefetchScalarGridSpec(
            num_scalar_prefetch=2,
            grid=(q_count,),
            in_specs=[
                pl.BlockSpec((2, bands, points), lambda q, p, h: (0, 0, 0), pipeline_mode=pl.Buffered(1)),
                pl.BlockSpec((1, 2, points), lambda q, p, h: (q0 + q, 0, 0)),
            ]
            + specs,
            out_specs=[
                pl.BlockSpec((1, 2, rows, width), lambda q, p, h: (q, 0, 0, 0)),
                pl.BlockSpec((1, 2, rows, width), lambda q, p, h: (q, 0, 0, 0)),
                pl.BlockSpec((1, 2, width, points), lambda q, p, h: (q, 0, 0, 0)),
            ],
            scratch_shapes=[
                pltpu.VMEM((2, bands, width), jnp.float32),
                pltpu.VMEM((2 * width, points), jnp.bfloat16),
            ],
        ),
        out_shape=[
            jax.ShapeDtypeStruct((q_count, 2, rows, width), jnp.bfloat16),
            jax.ShapeDtypeStruct((q_count, 2, rows, width), jnp.float32),
            jax.ShapeDtypeStruct((q_count, 2, width, points), jnp.bfloat16),
        ],
        compiler_params=pltpu.CompilerParams(vmem_limit_bytes=VMEM_LIMIT),
        cost_estimate=SMALL_COST,
    )(picks, half, *arrays)


def mix_kernel(chunk_count, density_scale, count_ref, field_ref, own_ref, *refs):
    weights = refs[:chunk_count]
    partners = refs[chunk_count:2 * chunk_count]
    source_ref, density_ref, left_real, left_imag, right = refs[-5:]
    bands = own_ref.shape[1]

    @pl.when(pl.program_id(0) == 0)
    def _():
        start = 0
        for weight in weights:
            width = weight.shape[3]
            near, far = pl.ds(start, width), pl.ds(start + width, width)
            start += 2 * width
            left_real[:, near] = weight[0, 0]
            left_real[:, far] = -weight[0, 1]
            left_imag[:, near] = weight[0, 1]
            left_imag[:, far] = weight[0, 0]

    start = 0
    for partner in partners:
        width = 2 * partner.shape[2]
        right[pl.ds(start, width), :] = partner[0].reshape(width, partner.shape[3])
        start += width
    u, v = field_ref[0, 0:1], field_ref[0, 1:2]
    a, b = own_ref[0].astype(jnp.float32), own_ref[1].astype(jnp.float32)
    applied_real = (u * a - v * b).astype(jnp.bfloat16).astype(jnp.float32)
    applied_imag = (u * b + v * a).astype(jnp.bfloat16).astype(jnp.float32)
    real = applied_real - jnp.dot(left_real[...], right[...], preferred_element_type=jnp.float32)
    imag = applied_imag - jnp.dot(left_imag[...], right[...], preferred_element_type=jnp.float32)
    source_ref[0, 0, 0] = real.astype(jnp.bfloat16)
    source_ref[0, 0, 1] = imag.astype(jnp.bfloat16)
    term = a * real + b * imag
    ids = lax.broadcasted_iota(jnp.int32, (bands, 1), 0)
    term = jnp.where(ids < count_ref[0], term, 0.0)
    density_ref[...] = density_scale * jnp.sum(term, axis=0, keepdims=True)


def mix(q, count, potential, orbitals, partners, weights, buffer, density_scale):
    q_total = potential.shape[0]
    _, bands, points = orbitals.shape
    block = points // 4
    specs = [
        pl.BlockSpec((1, 2, block), lambda i, c: (q, 0, i)),
        pl.BlockSpec((2, bands, block), lambda i, c: (0, 0, i)),
    ]
    arrays = [potential, orbitals]
    for at, weight in weights:
        specs.append(pl.BlockSpec((1, 2, bands, weight.shape[3]), lambda i, c, at=at: (at, 0, 0, 0)))
        arrays.append(weight)
    for at, partner in partners:
        specs.append(pl.BlockSpec((1, 2, partner.shape[2], block), lambda i, c, at=at: (at, 0, 0, i)))
        arrays.append(partner)
    aliases = {}
    if buffer is not None:
        specs.append(pl.BlockSpec(memory_space=pl.ANY))
        arrays.append(buffer)
        aliases = {len(arrays): 0}
    return pl.pallas_call(
        functools.partial(mix_kernel, len(weights), density_scale),
        grid_spec=pltpu.PrefetchScalarGridSpec(
            num_scalar_prefetch=1,
            grid=(points // block,),
            in_specs=specs,
            out_specs=[
                pl.BlockSpec((1, 1, 2, bands, block), lambda i, c: (q, 0, 0, 0, i)),
                pl.BlockSpec((1, block), lambda i, c: (0, i)),
            ],
            scratch_shapes=[pltpu.VMEM((bands, 2 * bands), jnp.bfloat16)] * 2
            + [pltpu.VMEM((2 * bands, block), jnp.bfloat16)],
        ),
        out_shape=[
            jax.ShapeDtypeStruct((q_total, 1, 2, bands, points), jnp.bfloat16),
            jax.ShapeDtypeStruct((1, points), jnp.float32),
        ],
        input_output_aliases=aliases,
        compiler_params=pltpu.CompilerParams(vmem_limit_bytes=VMEM_LIMIT),
        cost_estimate=SMALL_COST,
    )(count, *arrays)


def shards(orbitals, potential, partners, occupied):
    own = orbitals[0]
    bands, points = own.shape[1:]
    q_count = potential.shape[0]
    k_count = partners.shape[1]
    k_index = lax.axis_index("ka")
    g_index = lax.axis_index("grid")
    ka_bits = axis_bits("ka")[::-1]
    grid_bits = axis_bits("grid")
    volume_weight = 1.0 / (points * lax.axis_size("grid"))
    density_weight = 2.0 / (k_count * bands)
    k_table = jnp.arange(k_count, dtype=jnp.int32)
    partner_ids = jnp.sum((k_table == k_index) * partners, axis=1)
    partner_counts = jnp.sum((partner_ids[:, None] == k_table[None, :]) * occupied[None, :], axis=1)
    own_count = jnp.sum((k_table == k_index) * occupied)[None]
    picks = partner_ids ^ k_index
    last_bit = ka_bits[-1]

    fetched = []
    spans = [(first * bands // 4, count * bands // 4) for first, count, _ in PLAN]
    for start, width in spans:
        have = {0: own[:, start:start + width]}
        for bit in ka_bits[:-1]:
            for rel in list(have):
                have[rel ^ bit] = swap(have[rel], "ka", bit)
        fetched.append(have)
    sibling = swap(own, "ka", last_bit)

    def bit_of(bit):
        return (g_index // bit) % 2

    away_half = (1 - bit_of(grid_bits[0]))[None].astype(jnp.int32)

    groups = []
    for c, (_, _, together) in enumerate(PLAN):
        groups += [(c, 0, q_count)] if together else [(c, q, 1) for q in range(q_count)]
    state = {}
    picked = {}
    previous = own_count

    def run_overlap(i):
        nonlocal previous
        c, q0, count = groups[i]
        have = fetched[c]
        if q0 == 0:
            for rel in list(have):
                if rel:
                    have[rel ^ last_bit] = swap(after(have[rel], previous), "ka", last_bit)
            have[last_bit] = None
        sources = []
        for rel in range(len(have)):
            whole = {0: own, last_bit: sibling}.get(rel)
            sources.append((have[rel], False) if whole is None else (whole, True))
        leaving, keep, picked[i] = overlap(
            q0, count, spans[c][0], picks[q0:q0 + count], away_half, own, after(potential, previous), sources
        )
        previous = leaving
        state[i] = (keep, swap(leaving, "grid", grid_bits[0]))

    def run_scatter(i, bit, full):
        nonlocal previous
        keep, arriving = state[i]
        arriving = after(arriving, previous)
        mine = bit_of(bit)
        half = keep.shape[2] // 2

        def part(which):
            return lax.dynamic_slice_in_dim(keep, which * half, half, 2) + lax.dynamic_slice_in_dim(
                arriving, which * half, half, 2
            ).astype(jnp.float32)

        if full:
            leaving = (keep + arriving.astype(jnp.float32)).astype(jnp.bfloat16)
            kept = leaving
        else:
            leaving = part(1 - mine).astype(jnp.bfloat16)
            kept = part(mine)
        previous = leaving
        state[i] = (kept, swap(leaving, "grid", bit))

    def run_turn(i, bit):
        nonlocal previous
        c, q0, count = groups[i]
        start, width = spans[c]
        keep, arriving = state[i]
        total = keep.astype(jnp.float32) + after(arriving, previous).astype(jnp.float32)
        limits = partner_counts[q0:q0 + count][:, None, None, None]
        mask = (start + jnp.arange(width, dtype=jnp.int32)) < limits
        piece = jnp.where(mask, volume_weight * total, 0.0).astype(jnp.bfloat16)
        previous = piece
        state[i] = (piece, swap(piece, "grid", bit))

    def run_gather(i, done_bit, bit):
        nonlocal previous
        piece, other = state[i]
        upper = bit_of(done_bit) == 1
        other = after(other, previous) if bit is not None else other
        piece = jnp.concatenate([jnp.where(upper, other, piece), jnp.where(upper, piece, other)], axis=2)
        if bit is None:
            state[i] = piece
            return
        previous = piece
        state[i] = (piece, swap(piece, "grid", bit))

    stages = []
    steps = len(grid_bits)
    for i, (c, q0, count) in enumerate(groups):
        first, quarters, _ = PLAN[c]
        at = PACE * (first + quarters) + 0.2 * q0
        scale = quarters * count / q_count
        stages.append((at, i, functools.partial(run_overlap, i)))
        at += 0.85 * scale + LAG
        for s in range(1, steps):
            stages.append((at, i, functools.partial(run_scatter, i, grid_bits[s], s == steps - 1)))
            at += (0.4 if s < steps - 1 else 0.8) * scale + LAG
        stages.append((at, i, functools.partial(run_turn, i, grid_bits[steps - 2])))
        at += 0.4 * scale + LAG
        for s in range(steps - 2, 0, -1):
            stages.append((at, i, functools.partial(run_gather, i, grid_bits[s], grid_bits[s - 1])))
            at += 0.85 * scale + LAG
        stages.append((at, i, functools.partial(run_gather, i, grid_bits[0], None)))
    for _, _, stage in sorted(stages, key=lambda entry: entry[:2]):
        stage()

    buffer = None
    density = []
    for q in range(q_count):
        own_groups = [i for i, (_, q0, n) in enumerate(groups) if q0 <= q < q0 + n]
        weights = [(q - groups[i][1], state[i]) for i in own_groups]
        chosen = [(q - groups[i][1], picked[i]) for i in own_groups]
        buffer, term = mix(q, own_count, potential, own, chosen, weights, buffer, density_weight)
        density.append(term)
    density = jnp.concatenate(density, axis=0)
    parts = [density] + [swap(density, "ka", d) for d in range(1, lax.axis_size("ka"))]
    while len(parts) > 1:
        half = len(parts) // 2
        parts = [parts[i] + parts[i + half] for i in range(half)]
    return buffer, parts[0]


def solution(mesh):
    return jax.shard_map(
        shards,
        mesh=mesh,
        in_specs=(P("ka", None, None, "grid"), P(None, None, "grid"), P(), P()),
        out_specs=(P(None, "ka", None, None, "grid"), P(None, "grid")),
        check_vma=False,
    )
```

```python
import functools

import jax
import jax.numpy as jnp
from jax import lax
from jax.experimental import pallas as pl
from jax.experimental.pallas import tpu as pltpu
from jax.sharding import PartitionSpec as P

SMALL_COST = pl.CostEstimate(flops=1, bytes_accessed=1, transcendentals=0)
VMEM_LIMIT = 24 * 1024 * 1024
TRANSFERS = (2, 2)
KERNEL, NEAR, FAR, LATENCY = 0.4, 0.4, 0.8, 0.25
EARLY = 0.1
TIES = (1, 1, 1)
WAIT = 0.4
TURNED = ()


def swap(value, axis, bit):
    size = lax.axis_size(axis)
    return lax.ppermute(value, axis, [(i, i ^ bit) for i in range(size)])


def after(value, *others):
    return lax.optimization_barrier((value,) + others)[0]


def axis_bits(axis):
    size = lax.axis_size(axis)
    return [1 << b for b in range(size.bit_length() - 1)]


def overlap_kernel(offsets, picks_ref, half_ref, own_ref, field_ref, *refs):
    sources = refs[:-5]
    send_ref, keep_ref, pick_ref, full, turned = refs[-5:]
    pick = picks_ref[pl.program_id(0)]
    for j, first in enumerate(offsets):
        @pl.when(pick == j)
        def _():
            pick_ref[0] = sources[j][:, first:first + pick_ref.shape[2], :]
    _, bands, points = own_ref.shape
    width = pick_ref.shape[2]
    rows = bands // 2
    u, v = field_ref[0, 0:1], field_ref[0, 1:2]
    p_real, p_imag = pick_ref[0, 0].astype(jnp.float32), pick_ref[0, 1].astype(jnp.float32)
    turned[:width] = (u * p_real + v * p_imag).astype(jnp.bfloat16)
    turned[width:] = (u * p_imag - v * p_real).astype(jnp.bfloat16)
    both = lax.dot_general(
        own_ref[...].reshape(2 * bands, points),
        turned[...],
        (((1,), (1,)), ((), ())),
        preferred_element_type=jnp.float32,
    )
    full[0] = both[:bands, :width] + both[bands:, width:]
    full[1] = both[bands:, :width] - both[:bands, width:]
    away = pl.multiple_of(half_ref[0] * rows, rows)
    here = pl.multiple_of((1 - half_ref[0]) * rows, rows)
    send_ref[0] = full[:, pl.ds(away, rows), :].astype(send_ref.dtype)
    keep_ref[0] = full[:, pl.ds(here, rows), :]


def overlap(q0, q_count, width, picks, half, own, potential, sources):
    _, bands, points = own.shape
    rows = bands // 2
    in_vmem = pl.BlockSpec(memory_space=pltpu.VMEM)
    arrays = [own, potential] + [array for array, _ in sources]
    return pl.pallas_call(
        functools.partial(overlap_kernel, [offset for _, offset in sources]),
        grid_spec=pltpu.PrefetchScalarGridSpec(
            num_scalar_prefetch=2,
            grid=(q_count,),
            in_specs=[
                in_vmem,
                pl.BlockSpec((1, 2, points), lambda q, p, h: (q0 + q, 0, 0)),
            ]
            + [in_vmem] * len(sources),
            out_specs=[
                pl.BlockSpec((1, 2, rows, width), lambda q, p, h: (q, 0, 0, 0)),
                pl.BlockSpec((1, 2, rows, width), lambda q, p, h: (q, 0, 0, 0)),
                pl.BlockSpec((1, 2, width, points), lambda q, p, h: (q, 0, 0, 0)),
            ],
            scratch_shapes=[
                pltpu.VMEM((2, bands, width), jnp.float32),
                pltpu.VMEM((2 * width, points), jnp.bfloat16),
            ],
        ),
        out_shape=[
            jax.ShapeDtypeStruct((q_count, 2, rows, width), jnp.bfloat16),
            jax.ShapeDtypeStruct((q_count, 2, rows, width), jnp.float32),
            jax.ShapeDtypeStruct((q_count, 2, width, points), jnp.bfloat16),
        ],
        compiler_params=pltpu.CompilerParams(vmem_limit_bytes=VMEM_LIMIT),
        cost_estimate=SMALL_COST,
    )(picks, half, *arrays)


def mix_kernel(places, density_scale, count_ref, field_ref, own_ref, *refs):
    weights = refs[:len(places)]
    partners = refs[len(places):2 * len(places)]
    source_ref, density_ref, left_real, left_imag, right = refs[-5:]
    bands = own_ref.shape[1]

    @pl.when(pl.program_id(0) == 0)
    def _():
        start = 0
        for weight in weights:
            width = weight.shape[3]
            near, far = pl.ds(start, width), pl.ds(start + width, width)
            start += 2 * width
            left_real[:, near] = weight[0, 0]
            left_real[:, far] = -weight[0, 1]
            left_imag[:, near] = weight[0, 1]
            left_imag[:, far] = weight[0, 0]

    start = 0
    block = right.shape[1]
    here = pl.ds(pl.multiple_of(pl.program_id(0) * block, block), block)
    for at, partner in zip(places, partners):
        width = 2 * partner.shape[2]
        right[pl.ds(start, width), :] = partner[at, :, :, here].reshape(width, block)
        start += width
    u, v = field_ref[0, 0:1], field_ref[0, 1:2]
    a, b = own_ref[0, :, here].astype(jnp.float32), own_ref[1, :, here].astype(jnp.float32)
    applied_real = (u * a - v * b).astype(jnp.bfloat16).astype(jnp.float32)
    applied_imag = (u * b + v * a).astype(jnp.bfloat16).astype(jnp.float32)
    real = applied_real - jnp.dot(left_real[...], right[...], preferred_element_type=jnp.float32)
    imag = applied_imag - jnp.dot(left_imag[...], right[...], preferred_element_type=jnp.float32)
    source_ref[0, 0, 0] = real.astype(jnp.bfloat16)
    source_ref[0, 0, 1] = imag.astype(jnp.bfloat16)
    term = a * real + b * imag
    ids = lax.broadcasted_iota(jnp.int32, (bands, 1), 0)
    term = jnp.where(ids < count_ref[0], term, 0.0)
    density_ref[...] = density_scale * jnp.sum(term, axis=0, keepdims=True)


def mix(q, count, potential, orbitals, partners, weights, buffer, density_scale):
    q_total = potential.shape[0]
    _, bands, points = orbitals.shape
    block = points // 2
    in_vmem = pl.BlockSpec(memory_space=pltpu.VMEM)
    specs = [
        pl.BlockSpec((1, 2, block), lambda i, c: (q, 0, i)),
        in_vmem,
    ]
    arrays = [potential, orbitals]
    arrays += weights + [partner for _, partner in partners]
    specs += [in_vmem] * (len(weights) + len(partners))
    aliases = {}
    if buffer is not None:
        specs.append(pl.BlockSpec(memory_space=pl.ANY))
        arrays.append(buffer)
        aliases = {len(arrays): 0}
    return pl.pallas_call(
        functools.partial(mix_kernel, [at for at, _ in partners], density_scale),
        grid_spec=pltpu.PrefetchScalarGridSpec(
            num_scalar_prefetch=1,
            grid=(points // block,),
            in_specs=specs,
            out_specs=[
                pl.BlockSpec((1, 1, 2, bands, block), lambda i, c: (q, 0, 0, 0, i)),
                pl.BlockSpec((1, block), lambda i, c: (0, i)),
            ],
            scratch_shapes=[pltpu.VMEM((bands, 2 * bands), jnp.bfloat16)] * 2
            + [pltpu.VMEM((2 * bands, block), jnp.bfloat16)],
        ),
        out_shape=[
            jax.ShapeDtypeStruct((q_total, 1, 2, bands, points), jnp.bfloat16),
            jax.ShapeDtypeStruct((1, points), jnp.float32),
        ],
        input_output_aliases=aliases,
        compiler_params=pltpu.CompilerParams(vmem_limit_bytes=VMEM_LIMIT),
        cost_estimate=SMALL_COST,
    )(count, *arrays)


def shards(orbitals, potential, partners, occupied):
    own = orbitals[0]
    bands, points = own.shape[1:]
    q_count = potential.shape[0]
    k_count = partners.shape[1]
    k_index = lax.axis_index("ka")
    g_index = lax.axis_index("grid")
    ka_bits = axis_bits("ka")[::-1]
    grid_bits = axis_bits("grid")
    volume_weight = 1.0 / (points * lax.axis_size("grid"))
    density_weight = 2.0 / (k_count * bands)
    k_table = jnp.arange(k_count, dtype=jnp.int32)
    partner_ids = jnp.sum((k_table == k_index) * partners, axis=1)
    partner_counts = jnp.sum((partner_ids[:, None] == k_table[None, :]) * occupied[None, :], axis=1)
    own_count = jnp.sum((k_table == k_index) * occupied)[None]
    picks = partner_ids ^ k_index
    last_bit = ka_bits[-1]

    fetched = []
    quarter = bands // 4
    edges = [sum(TRANSFERS[:t]) for t in range(len(TRANSFERS) + 1)]
    for first, last in zip(edges, edges[1:]):
        start, width = first * quarter, (last - first) * quarter
        piece = own[:, start:start + width] if not fetched else after(own, fetched[0][0])[:, start:start + width]
        have = {0: piece}
        for bit in ka_bits[:-1]:
            for rel in list(have):
                have[rel ^ bit] = swap(have[rel], "ka", bit)
        fetched.append(have)
    sibling = swap(own, "ka", last_bit)

    def bit_of(bit):
        return (g_index // bit) % 2

    def order_of(i):
        if i in TURNED and len(grid_bits) > 2:
            return [grid_bits[1], grid_bits[0]] + grid_bits[2:]
        return grid_bits

    groups = []
    for t, (first, last) in enumerate(zip(edges, edges[1:])):
        groups += [(t, c, 0, q_count) for c in range(first, last)]
    state = {}
    picked = {}
    previous = own_count

    def run_overlap(i):
        nonlocal previous
        t, c, q0, count = groups[i]
        have = fetched[t]
        if last_bit not in have:
            for rel in list(have):
                if rel:
                    have[rel ^ last_bit] = swap(after(have[rel], previous), "ka", last_bit)
            have[0], have[last_bit] = own, sibling
        sources = []
        for rel in range(len(have)):
            offset = c if rel in (0, last_bit) else c - edges[t]
            sources.append((have[rel], offset * quarter))
        leaving, keep, picked[i] = overlap(
            q0, count, quarter, picks[q0:q0 + count], 1 - bit_of(order_of(i)[0])[None], own, after(potential, previous), sources
        )
        previous = leaving
        state[i] = (keep, swap(leaving, "grid", order_of(i)[0]))

    def run_scatter(i, bit, full):
        nonlocal previous
        keep, arriving = state[i]
        arriving = after(arriving, previous) if TIES[0] else arriving
        mine = bit_of(bit)
        half = keep.shape[2] // 2

        def part(which):
            return lax.dynamic_slice_in_dim(keep, which * half, half, 2) + lax.dynamic_slice_in_dim(
                arriving, which * half, half, 2
            ).astype(jnp.float32)

        if full:
            leaving = (keep + arriving.astype(jnp.float32)).astype(jnp.bfloat16)
            kept = leaving
        else:
            leaving = part(1 - mine).astype(jnp.bfloat16)
            kept = part(mine)
        previous = leaving
        state[i] = (kept, swap(leaving, "grid", bit))

    def run_turn(i, bit):
        nonlocal previous
        _, c, q0, count = groups[i]
        start, width = c * quarter, quarter
        keep, arriving = state[i]
        total = keep.astype(jnp.float32) + (after(arriving, previous) if TIES[1] else arriving).astype(jnp.float32)
        limits = partner_counts[q0:q0 + count][:, None, None, None]
        mask = (start + jnp.arange(width, dtype=jnp.int32)) < limits
        piece = jnp.where(mask, volume_weight * total, 0.0).astype(jnp.bfloat16)
        previous = piece
        state[i] = (piece, swap(piece, "grid", bit))

    def run_gather(i, done_bit, bit):
        nonlocal previous
        upper = bit_of(done_bit) == 1
        piece, other = state[i]
        other = after(other, previous) if bit is not None and TIES[2] else other
        piece = jnp.concatenate([jnp.where(upper, other, piece), jnp.where(upper, piece, other)], axis=2)
        if bit is None:
            state[i] = [piece[q:q + 1] for q in range(piece.shape[0])]
            return
        previous = piece
        if i == len(groups) - 1 and bit == order_of(i)[0]:
            parts = [piece[q:q + 1] for q in range(piece.shape[0])]
            state[i] = [(part, swap(part, "grid", bit)) for part in parts]
        else:
            state[i] = (piece, swap(piece, "grid", bit))

    stages = []
    steps = len(grid_bits)
    for i, (t, c, q0, count) in enumerate(groups):
        bits = order_of(i)
        at = edges[t + 1] + LATENCY + KERNEL * (c - edges[t])
        stages.append((at + EARLY, i, functools.partial(run_overlap, i)))
        at += KERNEL + FAR + WAIT + (FAR - KERNEL) * (c - edges[t])
        for s in range(1, steps):
            last = s == steps - 1
            stages.append((at, i, functools.partial(run_scatter, i, bits[s], last)))
            at += (FAR if last else NEAR) + LATENCY
        stages.append((at, i, functools.partial(run_turn, i, bits[steps - 2])))
        at += NEAR + LATENCY
        for s in range(steps - 2, 0, -1):
            stages.append((at, i, functools.partial(run_gather, i, bits[s], bits[s - 1])))
            at += FAR + LATENCY
        if i < len(groups) - 1:
            stages.append((at, i, functools.partial(run_gather, i, bits[0], None)))
    for _, _, stage in sorted(stages, key=lambda entry: entry[:2]):
        stage()

    buffer = None
    density = []
    for q in range(q_count):
        own_groups = [i for i, (_, _, q0, n) in enumerate(groups) if q0 <= q < q0 + n]
        weights = [state[i][q - groups[i][2]] for i in own_groups]
        piece, other = weights[-1]
        upper = bit_of(order_of(len(groups) - 1)[0]) == 1
        if density:
            other = after(other, density[-1])
        weights[-1] = jnp.concatenate([jnp.where(upper, other, piece), jnp.where(upper, piece, other)], axis=2)
        chosen = [(q - groups[i][2], picked[i]) for i in own_groups]
        buffer, term = mix(q, own_count, potential, own, chosen, weights, buffer, density_weight)
        density.append(term)
    density = jnp.concatenate(density, axis=0)
    parts = [density] + [swap(density, "ka", d) for d in range(1, lax.axis_size("ka"))]
    while len(parts) > 1:
        half = len(parts) // 2
        parts = [parts[i] + parts[i + half] for i in range(half)]
    return buffer, parts[0]


def solution(mesh):
    return jax.shard_map(
        shards,
        mesh=mesh,
        in_specs=(P("ka", None, None, "grid"), P(None, None, "grid"), P(), P()),
        out_specs=(P(None, "ka", None, None, "grid"), P(None, "grid")),
        check_vma=False,
    )
```

```python
import functools

import jax
import jax.numpy as jnp
from jax import lax
from jax.experimental import pallas as pl
from jax.experimental.pallas import tpu as pltpu
from jax.sharding import PartitionSpec as P

SMALL_COST = pl.CostEstimate(flops=1, bytes_accessed=1, transcendentals=0)
OVERLAP_VMEM = 8
MIX_VMEM = 14
TRANSFERS = (2, 2)
KERNEL, NEAR, FAR, LATENCY = 0.4, 0.4, 0.8, 0.25
EARLY = 0.1
WAIT = 0.4
PIECES, STEPS = 2, 2
KERNEL_SUMS = 1
TIES = (1, 1, 1)
TURNED = ()


def swap(value, axis, bit):
    size = lax.axis_size(axis)
    return lax.ppermute(value, axis, [(i, i ^ bit) for i in range(size)])


def after(value, *others):
    return lax.optimization_barrier((value,) + others)[0]


def axis_bits(axis):
    size = lax.axis_size(axis)
    return [1 << b for b in range(size.bit_length() - 1)]


def overlap_kernel(offsets, picks_ref, half_ref, own_ref, field_ref, *refs):
    sources = refs[:-5]
    send_ref, keep_ref, pick_ref, full, turned = refs[-5:]
    pick = picks_ref[pl.program_id(0)]
    for j, first in enumerate(offsets):
        @pl.when(pick == j)
        def _():
            pick_ref[0] = sources[j][:, first:first + pick_ref.shape[2], :]
    _, bands, points = own_ref.shape
    width = pick_ref.shape[2]
    rows = bands // 2
    u, v = field_ref[0, 0:1], field_ref[0, 1:2]
    p_real, p_imag = pick_ref[0, 0].astype(jnp.float32), pick_ref[0, 1].astype(jnp.float32)
    turned[:width] = (u * p_real + v * p_imag).astype(jnp.bfloat16)
    turned[width:] = (u * p_imag - v * p_real).astype(jnp.bfloat16)
    both = lax.dot_general(
        own_ref[...].reshape(2 * bands, points),
        turned[...],
        (((1,), (1,)), ((), ())),
        preferred_element_type=jnp.float32,
    )
    full[0] = both[:bands, :width] + both[bands:, width:]
    full[1] = both[bands:, :width] - both[:bands, width:]
    away = pl.multiple_of(half_ref[0] * rows, rows)
    here = pl.multiple_of((1 - half_ref[0]) * rows, rows)
    send_ref[0] = full[:, pl.ds(away, rows), :].astype(send_ref.dtype)
    keep_ref[0] = full[:, pl.ds(here, rows), :]


def overlap(q0, q_count, width, picks, half, own, potential, sources):
    _, bands, points = own.shape
    rows = bands // 2
    in_vmem = pl.BlockSpec(memory_space=pltpu.VMEM)
    arrays = [own, potential] + [array for array, _ in sources]
    return pl.pallas_call(
        functools.partial(overlap_kernel, [offset for _, offset in sources]),
        grid_spec=pltpu.PrefetchScalarGridSpec(
            num_scalar_prefetch=2,
            grid=(q_count,),
            in_specs=[
                in_vmem,
                pl.BlockSpec((1, 2, points), lambda q, p, h: (q0 + q, 0, 0)),
            ]
            + [in_vmem] * len(sources),
            out_specs=[
                pl.BlockSpec((1, 2, rows, width), lambda q, p, h: (q, 0, 0, 0)),
                pl.BlockSpec((1, 2, rows, width), lambda q, p, h: (q, 0, 0, 0)),
                pl.BlockSpec((1, 2, width, points), lambda q, p, h: (q, 0, 0, 0)),
            ],
            scratch_shapes=[
                pltpu.VMEM((2, bands, width), jnp.float32),
                pltpu.VMEM((2 * width, points), jnp.bfloat16),
            ],
        ),
        out_shape=[
            jax.ShapeDtypeStruct((q_count, 2, rows, width), jnp.bfloat16),
            jax.ShapeDtypeStruct((q_count, 2, rows, width), jnp.float32),
            jax.ShapeDtypeStruct((q_count, 2, width, points), jnp.bfloat16),
        ],
        compiler_params=pltpu.CompilerParams(vmem_limit_bytes=OVERLAP_VMEM << 20),
        cost_estimate=SMALL_COST,
    )(picks, half, *arrays)


def sum_kernel(half_ref, keep_ref, arriving_ref, *outs):
    if len(outs) == 1:
        outs[0][...] = (keep_ref[...] + arriving_ref[...].astype(jnp.float32)).astype(jnp.bfloat16)
        return
    rows = outs[0].shape[2]
    for out, part in zip(outs, (half_ref[0], 1 - half_ref[0])):
        at = pl.ds(pl.multiple_of(part * rows, rows), rows)
        out[...] = (keep_ref[:, :, at, :] + arriving_ref[:, :, at, :].astype(jnp.float32)).astype(out.dtype)


def partial_sum(keep, arriving, half, full):
    count, two, rows, width = keep.shape
    part = rows if full else rows // 2
    whole = pl.BlockSpec((1, two, rows, width), lambda q, h: (q, 0, 0, 0))
    out = pl.BlockSpec((1, two, part, width), lambda q, h: (q, 0, 0, 0))
    types = [jnp.bfloat16] if full else [jnp.bfloat16, jnp.float32]
    return pl.pallas_call(
        sum_kernel,
        grid_spec=pltpu.PrefetchScalarGridSpec(
            num_scalar_prefetch=1, grid=(count,), in_specs=[whole, whole], out_specs=[out] * len(types)
        ),
        out_shape=[jax.ShapeDtypeStruct((count, two, part, width), dtype) for dtype in types],
        compiler_params=pltpu.CompilerParams(vmem_limit_bytes=OVERLAP_VMEM << 20),
        cost_estimate=SMALL_COST,
    )(half, keep, arriving)


def mix_kernel(places, density_scale, count_ref, field_ref, own_ref, *refs):
    weights = refs[:len(places)]
    partners = refs[len(places):2 * len(places)]
    source_ref, density_ref, left, right = refs[-4:]
    bands = own_ref.shape[1]

    @pl.when(pl.program_id(0) == 0)
    def _():
        start = 0
        for weight in weights:
            width = weight.shape[3]
            near, far = pl.ds(start, width), pl.ds(start + width, width)
            start += 2 * width
            left[:bands, near] = weight[0, 0]
            left[:bands, far] = -weight[0, 1]
            left[bands:, near] = weight[0, 1]
            left[bands:, far] = weight[0, 0]

    start = 0
    block = right.shape[1]
    here = pl.ds(pl.multiple_of(pl.program_id(0) * block, block), block)
    for at, partner in zip(places, partners):
        width = 2 * partner.shape[2]
        right[pl.ds(start, width), :] = partner[at, :, :, here].reshape(width, block)
        start += width
    piece = block // PIECES
    keep = lax.broadcasted_iota(jnp.int32, (bands, 1), 0) < count_ref[0]
    for n in range(PIECES):
        at = pl.ds(n * piece, piece)
        there = pl.ds(pl.multiple_of(pl.program_id(0) * block + n * piece, piece), piece)
        u, v = field_ref[0, 0:1, at], field_ref[0, 1:2, at]
        a, b = own_ref[0, :, there].astype(jnp.float32), own_ref[1, :, there].astype(jnp.float32)
        applied_real = (u * a - v * b).astype(jnp.bfloat16).astype(jnp.float32)
        applied_imag = (u * b + v * a).astype(jnp.bfloat16).astype(jnp.float32)
        mixed = jnp.dot(left[...], right[:, at], preferred_element_type=jnp.float32)
        real = applied_real - mixed[:bands]
        imag = applied_imag - mixed[bands:]
        source_ref[0, 0, 0, :, at] = real.astype(jnp.bfloat16)
        source_ref[0, 0, 1, :, at] = imag.astype(jnp.bfloat16)
        term = jnp.where(keep, a * real + b * imag, 0.0)
        density_ref[:, at] = density_scale * jnp.sum(term, axis=0, keepdims=True)


def mix(q, count, potential, orbitals, partners, weights, buffer, density_scale):
    q_total = potential.shape[0]
    _, bands, points = orbitals.shape
    block = points // STEPS
    in_vmem = pl.BlockSpec(memory_space=pltpu.VMEM)
    specs = [
        pl.BlockSpec((1, 2, block), lambda i, c: (q, 0, i)),
        in_vmem,
    ]
    arrays = [potential, orbitals]
    arrays += weights + [partner for _, partner in partners]
    specs += [in_vmem] * (len(weights) + len(partners))
    aliases = {}
    if buffer is not None:
        specs.append(pl.BlockSpec(memory_space=pl.ANY))
        arrays.append(buffer)
        aliases = {len(arrays): 0}
    return pl.pallas_call(
        functools.partial(mix_kernel, [at for at, _ in partners], density_scale),
        grid_spec=pltpu.PrefetchScalarGridSpec(
            num_scalar_prefetch=1,
            grid=(points // block,),
            in_specs=specs,
            out_specs=[
                pl.BlockSpec((1, 1, 2, bands, block), lambda i, c: (q, 0, 0, 0, i)),
                pl.BlockSpec((1, block), lambda i, c: (0, i)),
            ],
            scratch_shapes=[
                pltpu.VMEM((2 * bands, 2 * bands), jnp.bfloat16),
                pltpu.VMEM((2 * bands, block), jnp.bfloat16),
            ],
        ),
        out_shape=[
            jax.ShapeDtypeStruct((q_total, 1, 2, bands, points), jnp.bfloat16),
            jax.ShapeDtypeStruct((1, points), jnp.float32),
        ],
        input_output_aliases=aliases,
        compiler_params=pltpu.CompilerParams(vmem_limit_bytes=MIX_VMEM << 20),
        cost_estimate=SMALL_COST,
    )(count, *arrays)


def shards(orbitals, potential, partners, occupied):
    own = orbitals[0]
    bands, points = own.shape[1:]
    q_count = potential.shape[0]
    k_count = partners.shape[1]
    k_index = lax.axis_index("ka")
    g_index = lax.axis_index("grid")
    ka_bits = axis_bits("ka")[::-1]
    grid_bits = axis_bits("grid")
    volume_weight = 1.0 / (points * lax.axis_size("grid"))
    density_weight = 2.0 / (k_count * bands)
    k_table = jnp.arange(k_count, dtype=jnp.int32)
    partner_ids = jnp.sum((k_table == k_index) * partners, axis=1)
    partner_counts = jnp.sum((partner_ids[:, None] == k_table[None, :]) * occupied[None, :], axis=1)
    own_count = jnp.sum((k_table == k_index) * occupied)[None]
    picks = partner_ids ^ k_index
    last_bit = ka_bits[-1]

    fetched = []
    quarter = bands // 4
    edges = [sum(TRANSFERS[:t]) for t in range(len(TRANSFERS) + 1)]
    for first, last in zip(edges, edges[1:]):
        start, width = first * quarter, (last - first) * quarter
        piece = own[:, start:start + width] if not fetched else after(own, fetched[0][0])[:, start:start + width]
        have = {0: piece}
        for bit in ka_bits[:-1]:
            for rel in list(have):
                have[rel ^ bit] = swap(have[rel], "ka", bit)
        fetched.append(have)
    sibling = swap(own, "ka", last_bit)

    def bit_of(bit):
        return (g_index // bit) % 2

    def order_of(i):
        if i in TURNED and len(grid_bits) > 2:
            return [grid_bits[1], grid_bits[0]] + grid_bits[2:]
        return grid_bits

    groups = []
    for t, (first, last) in enumerate(zip(edges, edges[1:])):
        groups += [(t, c, 0, q_count) for c in range(first, last)]
    state = {}
    picked = {}
    previous = own_count

    def run_overlap(i):
        nonlocal previous
        t, c, q0, count = groups[i]
        have = fetched[t]
        if last_bit not in have:
            for rel in list(have):
                if rel:
                    have[rel ^ last_bit] = swap(after(have[rel], previous), "ka", last_bit)
            have[0], have[last_bit] = own, sibling
        sources = []
        for rel in range(len(have)):
            offset = c if rel in (0, last_bit) else c - edges[t]
            sources.append((have[rel], offset * quarter))
        leaving, keep, picked[i] = overlap(
            q0, count, quarter, picks[q0:q0 + count], 1 - bit_of(order_of(i)[0])[None], own, after(potential, previous), sources
        )
        previous = leaving
        state[i] = (keep, swap(leaving, "grid", order_of(i)[0]))

    def run_scatter(i, bit, full):
        nonlocal previous
        keep, arriving = state[i]
        arriving = after(arriving, previous) if TIES[0] else arriving
        mine = bit_of(bit)
        half = keep.shape[2] // 2

        def part(which):
            return lax.dynamic_slice_in_dim(keep, which * half, half, 2) + lax.dynamic_slice_in_dim(
                arriving, which * half, half, 2
            ).astype(jnp.float32)

        if (KERNEL_SUMS >> full) & 1:
            leaving, *rest = partial_sum(keep, arriving, 1 - mine[None], full)
            kept = rest[0] if rest else leaving
        elif full:
            leaving = (keep + arriving.astype(jnp.float32)).astype(jnp.bfloat16)
            kept = leaving
        else:
            leaving = part(1 - mine).astype(jnp.bfloat16)
            kept = part(mine)
        previous = leaving
        state[i] = (kept, swap(leaving, "grid", bit))

    def run_turn(i, bit):
        nonlocal previous
        _, c, q0, count = groups[i]
        start, width = c * quarter, quarter
        keep, arriving = state[i]
        total = keep.astype(jnp.float32) + (after(arriving, previous) if TIES[1] else arriving).astype(jnp.float32)
        limits = partner_counts[q0:q0 + count][:, None, None, None]
        mask = (start + jnp.arange(width, dtype=jnp.int32)) < limits
        piece = jnp.where(mask, volume_weight * total, 0.0).astype(jnp.bfloat16)
        previous = piece
        state[i] = (piece, swap(piece, "grid", bit))

    def run_gather(i, done_bit, bit):
        nonlocal previous
        upper = bit_of(done_bit) == 1
        piece, other = state[i]
        other = after(other, previous) if bit is not None and TIES[2] else other
        piece = jnp.concatenate([jnp.where(upper, other, piece), jnp.where(upper, piece, other)], axis=2)
        if bit is None:
            state[i] = [piece[q:q + 1] for q in range(piece.shape[0])]
            return
        previous = piece
        if i == len(groups) - 1 and bit == order_of(i)[0]:
            parts = [piece[q:q + 1] for q in range(piece.shape[0])]
            state[i] = [(part, swap(part, "grid", bit)) for part in parts]
        else:
            state[i] = (piece, swap(piece, "grid", bit))

    stages = []
    steps = len(grid_bits)
    for i, (t, c, q0, count) in enumerate(groups):
        bits = order_of(i)
        at = edges[t + 1] + LATENCY + KERNEL * (c - edges[t])
        stages.append((at + EARLY, i, functools.partial(run_overlap, i)))
        at += KERNEL + FAR + WAIT + (FAR - KERNEL) * (c - edges[t])
        for s in range(1, steps):
            last = s == steps - 1
            stages.append((at, i, functools.partial(run_scatter, i, bits[s], last)))
            at += (FAR if last else NEAR) + LATENCY
        stages.append((at, i, functools.partial(run_turn, i, bits[steps - 2])))
        at += NEAR + LATENCY
        for s in range(steps - 2, 0, -1):
            stages.append((at, i, functools.partial(run_gather, i, bits[s], bits[s - 1])))
            at += FAR + LATENCY
        if i < len(groups) - 1:
            stages.append((at, i, functools.partial(run_gather, i, bits[0], None)))
    for _, _, stage in sorted(stages, key=lambda entry: entry[:2]):
        stage()

    buffer = None
    density = []
    for q in range(q_count):
        own_groups = [i for i, (_, _, q0, n) in enumerate(groups) if q0 <= q < q0 + n]
        weights = [state[i][q - groups[i][2]] for i in own_groups]
        piece, other = weights[-1]
        upper = bit_of(order_of(len(groups) - 1)[0]) == 1
        if density:
            other = after(other, density[-1])
        weights[-1] = jnp.concatenate([jnp.where(upper, other, piece), jnp.where(upper, piece, other)], axis=2)
        chosen = [(q - groups[i][2], picked[i]) for i in own_groups]
        buffer, term = mix(q, own_count, potential, own, chosen, weights, buffer, density_weight)
        density.append(term)
    density = jnp.concatenate(density, axis=0)
    parts = [density] + [swap(density, "ka", d) for d in range(1, lax.axis_size("ka"))]
    while len(parts) > 1:
        half = len(parts) // 2
        parts = [parts[i] + parts[i + half] for i in range(half)]
    return buffer, parts[0]


def solution(mesh):
    return jax.shard_map(
        shards,
        mesh=mesh,
        in_specs=(P("ka", None, None, "grid"), P(None, None, "grid"), P(), P()),
        out_specs=(P(None, "ka", None, None, "grid"), P(None, "grid")),
        check_vma=False,
    )
```

```python
import functools

import jax
import jax.numpy as jnp
from jax import lax
from jax.experimental import pallas as pl
from jax.experimental.pallas import tpu as pltpu
from jax.sharding import PartitionSpec as P

SMALL_COST = pl.CostEstimate(flops=1, bytes_accessed=1, transcendentals=0)
OVERLAP_VMEM = 8
MIX_VMEM = 14
TRANSFERS = (2, 2)
KERNEL, NEAR, FAR, LATENCY = 0.4, 0.4, 0.8, 0.25
EARLY = 0.1
WAIT = 0.4
PIECES, STEPS = 2, 2
KERNEL_SUMS = 1
TIES = (1, 1, 1)
TURNED = ()


def swap(value, axis, bit):
    size = lax.axis_size(axis)
    return lax.ppermute(value, axis, [(i, i ^ bit) for i in range(size)])


def after(value, *others):
    return lax.optimization_barrier((value,) + others)[0]


def axis_bits(axis):
    size = lax.axis_size(axis)
    return [1 << b for b in range(size.bit_length() - 1)]


def overlap_kernel(offsets, picks_ref, half_ref, own_ref, field_ref, *refs):
    sources = refs[:-5]
    send_ref, keep_ref, pick_ref, full, turned = refs[-5:]
    pick = picks_ref[pl.program_id(0)]
    for j, first in enumerate(offsets):
        @pl.when(pick == j)
        def _():
            pick_ref[0] = sources[j][:, first:first + pick_ref.shape[2], :]
    _, bands, points = own_ref.shape
    width = pick_ref.shape[2]
    rows = bands // 2
    u, v = field_ref[0, 0:1], field_ref[0, 1:2]
    p_real, p_imag = pick_ref[0, 0].astype(jnp.float32), pick_ref[0, 1].astype(jnp.float32)
    turned[:width] = (u * p_real + v * p_imag).astype(jnp.bfloat16)
    turned[width:] = (u * p_imag - v * p_real).astype(jnp.bfloat16)
    both = lax.dot_general(
        own_ref[...].reshape(2 * bands, points),
        turned[...],
        (((1,), (1,)), ((), ())),
        preferred_element_type=jnp.float32,
    )
    full[0] = both[:bands, :width] + both[bands:, width:]
    full[1] = both[bands:, :width] - both[:bands, width:]
    away = pl.multiple_of(half_ref[0] * rows, rows)
    here = pl.multiple_of((1 - half_ref[0]) * rows, rows)
    send_ref[0] = full[:, pl.ds(away, rows), :].astype(send_ref.dtype)
    keep_ref[0] = full[:, pl.ds(here, rows), :]


def overlap(q0, q_count, width, picks, half, own, potential, sources):
    _, bands, points = own.shape
    rows = bands // 2
    in_vmem = pl.BlockSpec(memory_space=pltpu.VMEM)
    arrays = [own, potential] + [array for array, _ in sources]
    return pl.pallas_call(
        functools.partial(overlap_kernel, [offset for _, offset in sources]),
        grid_spec=pltpu.PrefetchScalarGridSpec(
            num_scalar_prefetch=2,
            grid=(q_count,),
            in_specs=[
                in_vmem,
                pl.BlockSpec((1, 2, points), lambda q, p, h: (q0 + q, 0, 0)),
            ]
            + [in_vmem] * len(sources),
            out_specs=[
                pl.BlockSpec((1, 2, rows, width), lambda q, p, h: (q, 0, 0, 0)),
                pl.BlockSpec((1, 2, rows, width), lambda q, p, h: (q, 0, 0, 0)),
                pl.BlockSpec((1, 2, width, points), lambda q, p, h: (q, 0, 0, 0)),
            ],
            scratch_shapes=[
                pltpu.VMEM((2, bands, width), jnp.float32),
                pltpu.VMEM((2 * width, points), jnp.bfloat16),
            ],
        ),
        out_shape=[
            jax.ShapeDtypeStruct((q_count, 2, rows, width), jnp.bfloat16),
            jax.ShapeDtypeStruct((q_count, 2, rows, width), jnp.float32),
            jax.ShapeDtypeStruct((q_count, 2, width, points), jnp.bfloat16),
        ],
        compiler_params=pltpu.CompilerParams(vmem_limit_bytes=OVERLAP_VMEM << 20),
        cost_estimate=SMALL_COST,
    )(picks, half, *arrays)


def sum_kernel(half_ref, keep_ref, arriving_ref, *outs):
    if len(outs) == 1:
        outs[0][...] = (keep_ref[...] + arriving_ref[...].astype(jnp.float32)).astype(jnp.bfloat16)
        return
    rows = outs[0].shape[2]
    for out, part in zip(outs, (half_ref[0], 1 - half_ref[0])):
        at = pl.ds(pl.multiple_of(part * rows, rows), rows)
        out[...] = (keep_ref[:, :, at, :] + arriving_ref[:, :, at, :].astype(jnp.float32)).astype(out.dtype)


def partial_sum(keep, arriving, half, full):
    count, two, rows, width = keep.shape
    part = rows if full else rows // 2
    whole = pl.BlockSpec((1, two, rows, width), lambda q, h: (q, 0, 0, 0))
    out = pl.BlockSpec((1, two, part, width), lambda q, h: (q, 0, 0, 0))
    types = [jnp.bfloat16] if full else [jnp.bfloat16, jnp.float32]
    return pl.pallas_call(
        sum_kernel,
        grid_spec=pltpu.PrefetchScalarGridSpec(
            num_scalar_prefetch=1, grid=(count,), in_specs=[whole, whole], out_specs=[out] * len(types)
        ),
        out_shape=[jax.ShapeDtypeStruct((count, two, part, width), dtype) for dtype in types],
        compiler_params=pltpu.CompilerParams(vmem_limit_bytes=OVERLAP_VMEM << 20),
        cost_estimate=SMALL_COST,
    )(half, keep, arriving)


def mix_kernel(places, density_scale, count_ref, field_ref, own_ref, *refs):
    weights = refs[:len(places)]
    partners = refs[len(places):2 * len(places)]
    source_ref, density_ref, left, right = refs[-4:]
    bands = own_ref.shape[1]

    @pl.when(pl.program_id(0) == 0)
    def _():
        start = 0
        for weight in weights:
            width = weight.shape[3]
            near, far = pl.ds(start, width), pl.ds(start + width, width)
            start += 2 * width
            left[:bands, near] = weight[0, 0]
            left[:bands, far] = -weight[0, 1]
            left[bands:, near] = weight[0, 1]
            left[bands:, far] = weight[0, 0]

    start = 0
    block = right.shape[1]
    here = pl.ds(pl.multiple_of(pl.program_id(0) * block, block), block)
    for at, partner in zip(places, partners):
        width = 2 * partner.shape[2]
        right[pl.ds(start, width), :] = partner[at, :, :, here].reshape(width, block)
        start += width
    piece = block // PIECES
    keep = lax.broadcasted_iota(jnp.int32, (bands, 1), 0) < count_ref[0]
    for n in range(PIECES):
        at = pl.ds(n * piece, piece)
        there = pl.ds(pl.multiple_of(pl.program_id(0) * block + n * piece, piece), piece)
        u, v = field_ref[0, 0:1, at], field_ref[0, 1:2, at]
        a, b = own_ref[0, :, there].astype(jnp.float32), own_ref[1, :, there].astype(jnp.float32)
        applied_real = (u * a - v * b).astype(jnp.bfloat16).astype(jnp.float32)
        applied_imag = (u * b + v * a).astype(jnp.bfloat16).astype(jnp.float32)
        mixed = jnp.dot(left[...], right[:, at], preferred_element_type=jnp.float32)
        real = applied_real - mixed[:bands]
        imag = applied_imag - mixed[bands:]
        source_ref[0, 0, 0, :, at] = real.astype(jnp.bfloat16)
        source_ref[0, 0, 1, :, at] = imag.astype(jnp.bfloat16)
        term = jnp.where(keep, a * real + b * imag, 0.0)
        density_ref[:, at] = density_scale * jnp.sum(term, axis=0, keepdims=True)


def mix(q, count, potential, orbitals, partners, weights, buffer, density_scale):
    q_total = potential.shape[0]
    _, bands, points = orbitals.shape
    block = points // STEPS
    in_vmem = pl.BlockSpec(memory_space=pltpu.VMEM)
    specs = [
        pl.BlockSpec((1, 2, block), lambda i, c: (q, 0, i)),
        in_vmem,
    ]
    arrays = [potential, orbitals]
    arrays += weights + [partner for _, partner in partners]
    specs += [in_vmem] * (len(weights) + len(partners))
    aliases = {}
    if buffer is not None:
        specs.append(pl.BlockSpec(memory_space=pl.ANY))
        arrays.append(buffer)
        aliases = {len(arrays): 0}
    return pl.pallas_call(
        functools.partial(mix_kernel, [at for at, _ in partners], density_scale),
        grid_spec=pltpu.PrefetchScalarGridSpec(
            num_scalar_prefetch=1,
            grid=(points // block,),
            in_specs=specs,
            out_specs=[
                pl.BlockSpec((1, 1, 2, bands, block), lambda i, c: (q, 0, 0, 0, i)),
                pl.BlockSpec((1, block), lambda i, c: (0, i)),
            ],
            scratch_shapes=[
                pltpu.VMEM((2 * bands, 2 * bands), jnp.bfloat16),
                pltpu.VMEM((2 * bands, block), jnp.bfloat16),
            ],
        ),
        out_shape=[
            jax.ShapeDtypeStruct((q_total, 1, 2, bands, points), jnp.bfloat16),
            jax.ShapeDtypeStruct((1, points), jnp.float32),
        ],
        input_output_aliases=aliases,
        compiler_params=pltpu.CompilerParams(vmem_limit_bytes=MIX_VMEM << 20),
        cost_estimate=SMALL_COST,
    )(count, *arrays)


def shards(orbitals, potential, partners, occupied):
    own = orbitals[0]
    bands, points = own.shape[1:]
    q_count = potential.shape[0]
    k_count = partners.shape[1]
    k_index = lax.axis_index("ka")
    g_index = lax.axis_index("grid")
    ka_bits = axis_bits("ka")[::-1]
    grid_bits = axis_bits("grid")
    volume_weight = 1.0 / (points * lax.axis_size("grid"))
    density_weight = 2.0 / (k_count * bands)
    k_table = jnp.arange(k_count, dtype=jnp.int32)
    partner_ids = jnp.sum((k_table == k_index) * partners, axis=1)
    partner_counts = jnp.sum((partner_ids[:, None] == k_table[None, :]) * occupied[None, :], axis=1)
    own_count = jnp.sum((k_table == k_index) * occupied)[None]
    picks = partner_ids ^ k_index
    last_bit = ka_bits[-1]

    fetched = []
    quarter = bands // 4
    edges = [sum(TRANSFERS[:t]) for t in range(len(TRANSFERS) + 1)]
    for first, last in zip(edges, edges[1:]):
        start, width = first * quarter, (last - first) * quarter
        piece = own[:, start:start + width] if not fetched else after(own, fetched[0][0])[:, start:start + width]
        have = {0: piece}
        for bit in ka_bits[:-1]:
            for rel in list(have):
                have[rel ^ bit] = swap(have[rel], "ka", bit)
        fetched.append(have)
    sibling = swap(own, "ka", last_bit)

    def bit_of(bit):
        return (g_index // bit) % 2

    def order_of(i):
        if i in TURNED and len(grid_bits) > 2:
            return [grid_bits[1], grid_bits[0]] + grid_bits[2:]
        return grid_bits

    groups = []
    for t, (first, last) in enumerate(zip(edges, edges[1:])):
        groups += [(t, c, 0, q_count) for c in range(first, last)]
    state = {}
    picked = {}
    previous = own_count

    def run_overlap(i):
        nonlocal previous
        t, c, q0, count = groups[i]
        have = fetched[t]
        if last_bit not in have:
            for rel in list(have):
                if rel:
                    have[rel ^ last_bit] = swap(after(have[rel], previous), "ka", last_bit)
            have[0], have[last_bit] = own, sibling
        sources = []
        for rel in range(len(have)):
            offset = c if rel in (0, last_bit) else c - edges[t]
            sources.append((have[rel], offset * quarter))
        leaving, keep, picked[i] = overlap(
            q0, count, quarter, picks[q0:q0 + count], 1 - bit_of(order_of(i)[0])[None], own, after(potential, previous), sources
        )
        previous = leaving
        state[i] = (keep, swap(leaving, "grid", order_of(i)[0]))

    def run_scatter(i, bit, full):
        nonlocal previous
        keep, arriving = state[i]
        arriving = after(arriving, previous) if TIES[0] else arriving
        mine = bit_of(bit)
        half = keep.shape[2] // 2

        def part(which):
            return lax.dynamic_slice_in_dim(keep, which * half, half, 2) + lax.dynamic_slice_in_dim(
                arriving, which * half, half, 2
            ).astype(jnp.float32)

        if (KERNEL_SUMS >> full) & 1:
            leaving, *rest = partial_sum(keep, arriving, 1 - mine[None], full)
            kept = rest[0] if rest else leaving
        elif full:
            leaving = (keep + arriving.astype(jnp.float32)).astype(jnp.bfloat16)
            kept = leaving
        else:
            leaving = part(1 - mine).astype(jnp.bfloat16)
            kept = part(mine)
        previous = leaving
        state[i] = (kept, swap(leaving, "grid", bit))

    def run_turn(i, bit):
        nonlocal previous
        _, c, q0, count = groups[i]
        start, width = c * quarter, quarter
        keep, arriving = state[i]
        total = keep.astype(jnp.float32) + (after(arriving, previous) if TIES[1] else arriving).astype(jnp.float32)
        limits = partner_counts[q0:q0 + count][:, None, None, None]
        mask = (start + jnp.arange(width, dtype=jnp.int32)) < limits
        piece = jnp.where(mask, volume_weight * total, 0.0).astype(jnp.bfloat16)
        previous = piece
        state[i] = (piece, swap(piece, "grid", bit))

    def run_gather(i, done_bit, bit):
        nonlocal previous
        upper = bit_of(done_bit) == 1
        piece, other = state[i]
        other = after(other, previous) if bit is not None and TIES[2] else other
        piece = jnp.concatenate([jnp.where(upper, other, piece), jnp.where(upper, piece, other)], axis=2)
        if bit is None:
            state[i] = [piece[q:q + 1] for q in range(piece.shape[0])]
            return
        previous = piece
        if i == len(groups) - 1 and bit == order_of(i)[0]:
            state[i] = []
            for part in (piece[:1], piece[1:]):
                if part.shape[0]:
                    other = swap(part, "grid", bit)
                    state[i] += [(part[q:q + 1], other[q:q + 1]) for q in range(part.shape[0])]
        else:
            state[i] = (piece, swap(piece, "grid", bit))

    stages = []
    steps = len(grid_bits)
    for i, (t, c, q0, count) in enumerate(groups):
        bits = order_of(i)
        at = edges[t + 1] + LATENCY + KERNEL * (c - edges[t])
        stages.append((at + EARLY, i, functools.partial(run_overlap, i)))
        at += KERNEL + FAR + WAIT + (FAR - KERNEL) * (c - edges[t])
        for s in range(1, steps):
            last = s == steps - 1
            stages.append((at, i, functools.partial(run_scatter, i, bits[s], last)))
            at += (FAR if last else NEAR) + LATENCY
        stages.append((at, i, functools.partial(run_turn, i, bits[steps - 2])))
        at += NEAR + LATENCY
        for s in range(steps - 2, 0, -1):
            stages.append((at, i, functools.partial(run_gather, i, bits[s], bits[s - 1])))
            at += FAR + LATENCY
        if i < len(groups) - 1:
            stages.append((at, i, functools.partial(run_gather, i, bits[0], None)))
    for _, _, stage in sorted(stages, key=lambda entry: entry[:2]):
        stage()

    buffer = None
    density = []
    for q in range(q_count):
        own_groups = [i for i, (_, _, q0, n) in enumerate(groups) if q0 <= q < q0 + n]
        weights = [state[i][q - groups[i][2]] for i in own_groups]
        piece, other = weights[-1]
        upper = bit_of(order_of(len(groups) - 1)[0]) == 1
        if density:
            other = after(other, density[-1])
        weights[-1] = jnp.concatenate([jnp.where(upper, other, piece), jnp.where(upper, piece, other)], axis=2)
        chosen = [(q - groups[i][2], picked[i]) for i in own_groups]
        buffer, term = mix(q, own_count, potential, own, chosen, weights, buffer, density_weight)
        density.append(term)
    density = jnp.concatenate(density, axis=0)
    parts = [density] + [swap(density, "ka", d) for d in range(1, lax.axis_size("ka"))]
    while len(parts) > 1:
        half = len(parts) // 2
        parts = [parts[i] + parts[i + half] for i in range(half)]
    return buffer, parts[0]


def solution(mesh):
    return jax.shard_map(
        shards,
        mesh=mesh,
        in_specs=(P("ka", None, None, "grid"), P(None, None, "grid"), P(), P()),
        out_specs=(P(None, "ka", None, None, "grid"), P(None, "grid")),
        check_vma=False,
    )
```
